32 devices in a mesh: site: 8 (over z, y), sector: 4 (over x, core).
Axes of the slice: x: 2, y: 2, z: 4, core: 2. Of those that a mesh axis runs over, the one named last changes fastest.
Arguments:
- top_blocks: bfloat16 [8, 32, 512, 512], P('site', 'sector'), may hold values from -0.06363961 to 0.06363961
- bottom_blocks: bfloat16 [8, 32, 512, 512], P('site', 'sector'), may hold values from -0.06363961 to 0.06363961
- row_tensor: bfloat16 [8, 32, 512, 128], P('site', 'sector'), may hold values from -0.25 to 0.25
- merge_owner: int32 [8, 32, 1], P('site', 'sector'), may hold values from 0 to 3; in each aligned block of 8 rows (0 to 7, 8 to 15, ..., all dimensions but the last counted through in order) at most 4 rows name the same one
- merge_sub: int32 [8, 32], P('site', 'sector'), may hold values from 0 to 1
Outputs:
- top_canonical: float32 [8, 8, 128, 512], P('site', 'sector')
- bottom_canonical: float32 [8, 8, 128, 512], P('site', 'sector')
The draws below stay inside these ranges and needn't reach their ends.
Inputs may be any that keep to these rules, and one draw needn't show every extreme that they name: `merge_owner`: among the 8 blocks of one device, at most 4 name one owner, a bound that some block reaches.
All inputs are finite; a program needn't handle non-finite values.
Results may differ from the reference program's by a relative error of at most 0.0014.
Values may be sent and summed in bfloat16 or wider, within the bound.
A program may use at most 64 MiB of HBM per device.

```python
import math
import jax
import jax.numpy as jnp
import numpy as np
from jax import lax

PH = 4
BD = 128
KD = 512
SEC_DEV = 2
NB_DEV = 8
CAP = 4
SITES = 8
NQ = 8
NBLK = 32
N_SECTOR = 4


def row_scales(leading_scale, other_scale):
    rows = jnp.arange(PH * BD, dtype=jnp.int32)
    return jnp.where(rows < BD, leading_scale, other_scale).astype(jnp.float32)[:, None]


def draw_top_blocks(key, part):
    key = jax.random.fold_in(key, 11)
    shape = (SITES, NBLK, PH * BD, KD)
    leading_scale = 0.12 / math.sqrt(BD)
    other_scale = 0.05 / math.sqrt(BD)
    random_part = jax.random.truncated_normal(key, -6.0, 6.0, shape, jnp.float32)
    return (random_part * row_scales(leading_scale, other_scale)).astype(jnp.bfloat16)


def draw_bottom_blocks(key, part):
    key = jax.random.fold_in(key, 23)
    shape = (SITES, NBLK, PH * BD, KD)
    leading_scale = 0.12 / math.sqrt(BD)
    other_scale = 0.05 / math.sqrt(BD)
    random_part = jax.random.truncated_normal(key, -6.0, 6.0, shape, jnp.float32)
    return (random_part * row_scales(leading_scale, other_scale)).astype(jnp.bfloat16)


def touch_ends(values, own_key, least, high):
    longest = values.shape.index(max(values.shape))
    spots = []
    for shift in (0, 1):
        where = [jax.random.randint(jax.random.fold_in(own_key, axis), (), 0, length) for axis, length in enumerate(values.shape)]
        where[longest] = (where[longest] + shift) % values.shape[longest]
        spots.append(tuple(where))
    return values.at[spots[0]].set(least).at[spots[1]].set(high)


def block_levels(key, extent, split, least, largest):
    loudness, own = 1.0, jax.random.fold_in(key, 6)
    for axis_at, blocks in split:
        draws = jnp.exp(jax.random.uniform(jax.random.fold_in(own, axis_at), (blocks,), jnp.float32, least / len(split), largest / len(split)))
        loudness = loudness * jnp.repeat(draws, extent[axis_at] // blocks).reshape([-1 if axis == axis_at else 1 for axis in range(len(extent))])
    return loudness


def assign_block(own_key, own, number, rows, amount, top, most, skew):
    sequence = jax.random.permutation(own_key, amount)
    crowded, common = shares(amount, rows * top, most, skew, True), shares(amount, rows * top, most, skew, False)
    places = jnp.arange(amount)

    def named(sizes, offset_by):
        used = int((sizes > 0).sum())
        fixed = max(1, used // 4)
        moved = fixed + (places - fixed + offset_by * (used - fixed)) % max(1, amount - fixed)
        return jnp.zeros((amount,), jnp.int32).at[sequence[jnp.where(places < fixed, places, moved)]].set(jnp.asarray(sizes, jnp.int32))

    sizes = jnp.where(number % 4 == 0, named(crowded, number // 4), named(common, number - number // 4 - 1))
    mixed = jax.random.permutation(jax.random.fold_in(own, 3), amount)
    giver, receiver = mixed[0:amount // 2 * 2:2], mixed[1:amount // 2 * 2:2]
    room = jnp.minimum(sizes[giver] - 1, most - sizes[receiver]) // 2
    room = jnp.where((giver == sequence[0]) | (receiver == sequence[0]) | (sizes[receiver] == 0), 0, jnp.maximum(room, 0))
    moved = jax.random.randint(jax.random.fold_in(own, 4), (amount // 2,), 0, 1 << 20) % (room + 1)
    sizes = sizes.at[giver].add(-moved).at[receiver].add(moved)
    members = jnp.searchsorted(jnp.cumsum(sizes), jnp.arange(rows * top), side="right").astype(jnp.int32)
    listing = members.reshape(top, rows).T
    listing = listing[jax.random.permutation(jax.random.fold_in(own, 1), rows)]
    offset_by = jax.random.randint(jax.random.fold_in(own, 2), (rows, 1), 0, top)
    return jnp.take_along_axis(listing, (jnp.arange(top)[None, :] + offset_by) % top, axis=1)


def shares(amount, total, most, skew, full):
    weights = [(1 << 20) // math.isqrt(grade ** skew) + 1 for grade in range(1, amount + 1)]
    largest = most if full else min(most, max(-(-total // amount), total * weights[0] // sum(weights)))
    least = 1 if total - largest >= amount - 1 else 0
    given, rest = [largest] + [least] * (amount - 1), total - largest - least * (amount - 1)
    while rest > 0:
        movable = [i for i in range(1, amount) if given[i] < largest] or [i for i in range(1, amount) if given[i] < most]
        whole, remaining = sum([weights[i] for i in movable]), rest
        for i in movable:
            extra = min(most - given[i], max(1, remaining * weights[i] // whole), rest)
            given[i] = given[i] + extra
            rest = rest - extra
    return np.array(given)


def gaussian(stream_key, shape, deviation, bound, cuts=(), kind=jnp.bfloat16):
    level = block_levels(stream_key, shape, cuts, -0.22, 0.18) if cuts else 1.0
    array = jax.random.normal(stream_key, shape, jnp.float32) * deviation * level
    return jnp.minimum(jnp.maximum(array, -bound), bound).astype(kind)


def setup_inputs(seed: int = 0) -> dict:
    key_of = jax.random.split(jax.random.key(seed), 6)
    top_blocks = draw_top_blocks(jax.random.fold_in(key_of[5], 71), 0)
    bottom_blocks = draw_bottom_blocks(jax.random.fold_in(key_of[5], 71), 0)
    row_tensor = gaussian(key_of[2], (SITES, NBLK, KD, BD), KD ** -0.5, 0.25, ((0, 8), (1, 4)))
    merge_owner_keys = jax.random.split(jax.random.fold_in(key_of[3], 1), SITES * NBLK // NB_DEV)
    merge_owner_turns = jax.random.permutation(jax.random.fold_in(key_of[3], 3), SITES * NBLK // NB_DEV)
    merge_owner = jax.vmap(lambda own, number: assign_block(jax.random.fold_in(key_of[3], 2), own, number, NB_DEV, N_SECTOR, 1, CAP, 2))(merge_owner_keys, merge_owner_turns).reshape((SITES, NBLK, 1))
    merge_sub = touch_ends(jax.random.randint(key_of[4], (SITES, NBLK), 0, SEC_DEV), jax.random.fold_in(key_of[4], 1), 0, SEC_DEV - 1).astype(jnp.int32)
    return dict(top_blocks=top_blocks, bottom_blocks=bottom_blocks, row_tensor=row_tensor, merge_owner=merge_owner, merge_sub=merge_sub)


def advance(carried, merged):
    grown = jnp.einsum('ulm,upmr->uplr', carried, merged, precision=lax.Precision.HIGHEST)
    gram = jnp.einsum('upla,uplb->uab', grown, grown, precision=lax.Precision.HIGHEST)
    lower = jnp.linalg.cholesky(gram)
    upper = jnp.swapaxes(lower, 1, 2)
    factor = lax.rsqrt(lax.optimization_barrier(jnp.mean(upper * upper, axis=(1, 2), keepdims=True)) + 1e-06)
    return (grown, lower, upper * factor)

def finish(grown, lower):
    count = grown.shape[0]
    turned = jnp.transpose(grown, (0, 3, 1, 2)).reshape(count, BD, PH * BD)
    return lax.linalg.triangular_solve(lower, turned, left_side=True, lower=True)

def merge_site(blocks, weights, target):
    absorbed = jnp.einsum('jkc,jcr->jkr', blocks.astype(jnp.float32), weights.astype(jnp.float32)).astype(jnp.bfloat16)
    table = (jnp.arange(NQ, dtype=jnp.int32)[:, None] == target[None, :]).astype(jnp.float32)
    merged = jnp.einsum('qj,jkr->qkr', table, absorbed.astype(jnp.float32)).reshape(NQ, PH, BD, BD)
    return merged.at[:, 0].add(jnp.eye(BD, dtype=jnp.float32))

def sweep_boundary(merged_all):
    start = jnp.broadcast_to(jnp.eye(BD, dtype=jnp.float32), (NQ, BD, BD))

    def step(carried, merged):
        grown, lower, following = advance(carried, merged)
        return (following, finish(grown, lower))
    unused, result = lax.scan(step, start, merged_all)
    return result

def reference(top_blocks, bottom_blocks, row_tensor, merge_owner, merge_sub):
    target = (merge_owner[:, :, 0] * SEC_DEV + merge_sub).astype(jnp.int32)
    merged_top = lax.map(lambda item: merge_site(item[0], item[1], item[2]), (top_blocks, row_tensor, target))
    merged_bottom = lax.map(lambda item: merge_site(item[0], item[1], item[2]), (bottom_blocks, row_tensor, target))
    return (sweep_boundary(merged_top), sweep_boundary(merged_bottom))
```

```python
import functools

import jax
import jax.numpy as jnp
from jax import lax
from jax.experimental import pallas as pl
from jax.experimental.pallas import tpu as pltpu
from jax.sharding import PartitionSpec as P

PH = 4
BD = 128
SEC_DEV = 2
CHAINS = 4
PANEL = 32
WIDTH = 4
HIGHEST = lax.Precision.HIGHEST
NT = (((1,), (1,)), ((), ()))


def mm(a, b):
    return jnp.dot(a, b, precision=HIGHEST, preferred_element_type=jnp.float32)


def mm_nt(a, b):
    return lax.dot_general(a, b, NT, precision=HIGHEST, preferred_element_type=jnp.float32)


def mm_tn(a, b):
    return lax.dot_general(
        a, b, (((0,), (0,)), ((), ())), precision=HIGHEST, preferred_element_type=jnp.float32
    )


def absorb_kernel(target, top, bottom, weights, partial):
    step = pl.program_id(0)

    @pl.when(step == 0)
    def _():
        partial[...] = jnp.zeros_like(partial)

    sector = target[step]
    for boundary, blocks in enumerate((top, bottom)):
        absorbed = jnp.dot(blocks[0, 0], weights[0, 0], preferred_element_type=jnp.float32)
        partial[sector, boundary] += absorbed.astype(jnp.bfloat16).astype(jnp.float32)


def absorb(target, top_blocks, bottom_blocks, row_tensor, sectors):
    count, rows, inner = top_blocks.shape[1:]
    block = lambda *tail: pl.BlockSpec((1, 1) + tail, lambda j, t: (0, j, 0, 0))
    return pl.pallas_call(
        absorb_kernel,
        out_shape=jax.ShapeDtypeStruct((sectors, 2, rows, BD), jnp.float32),
        grid_spec=pltpu.PrefetchScalarGridSpec(
            num_scalar_prefetch=1,
            grid=(count,),
            in_specs=[block(rows, inner), block(rows, inner), block(inner, BD)],
            out_specs=pl.BlockSpec((sectors, 2, rows, BD), lambda j, t: (0, 0, 0, 0)),
        ),
        compiler_params=pltpu.CompilerParams(vmem_limit_bytes=48 * 2**20),
        name="absorb",
    )(target, top_blocks, bottom_blocks, row_tensor)


def identity():
    return (
        lax.broadcasted_iota(jnp.int32, (BD, BD), 0) == lax.broadcasted_iota(jnp.int32, (BD, BD), 1)
    ).astype(jnp.float32)


def sweep_kernel(
    sites, owners, partial, m_out, x_out, g_out,
    own, near, away, landed, leaving, arriving, turned,
    own_sem, near_send, near_recv, away_send, away_recv, site_send, site_recv,
):
    chips = owners // 2
    site = lax.axis_index("site")
    sector = lax.axis_index("sector")
    core = sector % 2
    chip = sector // 2

    def at(site_to, sector_to):
        return (site_to, sector_to)

    partner = at(site, chip * 2 + (1 - core))

    def mate(shift):
        return at(site, ((chip + shift) % chips) * 2 + core)

    barrier = pltpu.get_barrier_semaphore()
    for device in [partner] + [mate(shift) for shift in range(1, chips)]:
        pl.semaphore_signal(barrier, inc=1, device_id=device, device_id_type=pl.DeviceIdType.MESH)

    @pl.when(site > 0)
    def _():
        pl.semaphore_signal(
            barrier, inc=1, device_id=at(site - 1, sector), device_id_type=pl.DeviceIdType.MESH
        )

    @pl.when(site < sites - 1)
    def _():
        pl.semaphore_signal(
            barrier, inc=1, device_id=at(site + 1, sector), device_id_type=pl.DeviceIdType.MESH
        )

    sides = jnp.where(site > 0, 1, 0) + jnp.where(site < sites - 1, 1, 0)
    pl.semaphore_wait(barrier, chips + sides)

    def own_copy(shift, k):
        owner = ((chip + shift) % chips) * 2 + core
        return pltpu.make_async_copy(partial.at[owner, k], own.at[shift, k], own_sem.at[shift, k])

    def near_copy(shift, k):
        owner = ((chip + shift) % chips) * 2 + (1 - core)
        return pltpu.make_async_remote_copy(
            src_ref=partial.at[owner, k], dst_ref=near.at[shift, k],
            send_sem=near_send.at[shift, k], recv_sem=near_recv.at[shift, k],
            device_id=partner, device_id_type=pl.DeviceIdType.MESH,
        )

    def away_copy(shift, k):
        return pltpu.make_async_remote_copy(
            src_ref=away.at[shift - 1, k], dst_ref=landed.at[shift - 1, k],
            send_sem=away_send.at[shift - 1, k], recv_sem=away_recv.at[shift - 1, k],
            device_id=mate(shift), device_id_type=pl.DeviceIdType.MESH,
        )

    def site_copy(k):
        return pltpu.make_async_remote_copy(
            src_ref=leaving.at[k], dst_ref=arriving.at[k],
            send_sem=site_send.at[k], recv_sem=site_recv.at[k],
            device_id=at(site + 1, sector), device_id_type=pl.DeviceIdType.MESH,
        )

    order = list(range(1, chips)) + [0]
    for shift in order:
        @pl.loop(0, CHAINS)
        def _(k):
            near_copy(shift, k).start()
            own_copy(shift, k).start()

    @pl.loop(0, CHAINS)
    def _(k):
        for shift in range(1, chips):
            near_copy(shift, k).wait_recv()
            own_copy(shift, k).wait()
            away[shift - 1, k] = (near[shift, k] + own[shift, k]).astype(jnp.bfloat16)
            away_copy(shift, k).start()

    eye = identity()

    @pl.loop(0, CHAINS)
    def _(k):
        near_copy(0, k).wait_recv()
        own_copy(0, k).wait()
        for shift in range(1, chips):
            away_copy(shift, k).wait_recv()
        for p in range(PH):
            rows = pl.ds(p * BD, BD)
            merged = near[0, k, rows, :] + own[0, k, rows, :]
            for shift in range(1, chips):
                merged += landed[shift - 1, k, rows, :].astype(jnp.float32)
            if p == 0:
                merged += eye
            m_out[k, rows, :] = merged
            turned[rows, :] = merged.T

        @pl.when(site == 0)
        def _():
            x_out[k] = eye

        @pl.when(site > 0)
        def _():
            site_copy(k).wait_recv()
            x_out[k] = arriving[k]

        half = mm(turned[...], x_out[k])
        gram = mm(half[:BD], m_out[k, pl.ds(0, BD), :])
        for p in range(1, PH):
            gram += mm(half[p * BD:(p + 1) * BD], m_out[k, pl.ds(p * BD, BD), :])
        g_out[k] = gram

        @pl.when(site < sites - 1)
        def _():
            trace = jnp.sum(jnp.sum(gram * eye, axis=0, keepdims=True), axis=1, keepdims=True)
            leaving[k] = gram / (trace * (1.0 / (BD * BD)) + 1e-06)
            site_copy(k).start()

    @pl.loop(0, CHAINS)
    def _(k):
        for shift in range(chips):
            near_copy(shift, k).wait_send()
        for shift in range(1, chips):
            away_copy(shift, k).wait_send()

        @pl.when(site < sites - 1)
        def _():
            site_copy(k).wait_send()


def sweep(partial, sites, owners):
    chips = owners // 2
    rows = PH * BD
    vmem = pl.BlockSpec(memory_space=pltpu.VMEM)
    f32 = jnp.float32
    dma = pltpu.SemaphoreType.DMA
    return pl.pallas_call(
        functools.partial(sweep_kernel, sites, owners),
        out_shape=(
            jax.ShapeDtypeStruct((CHAINS, rows, BD), f32),
            jax.ShapeDtypeStruct((CHAINS, BD, BD), f32),
            jax.ShapeDtypeStruct((CHAINS, BD, BD), f32),
        ),
        in_specs=[pl.BlockSpec(memory_space=pl.ANY)],
        out_specs=(vmem, vmem, vmem),
        scratch_shapes=[
            pltpu.VMEM((chips, CHAINS, rows, BD), f32),
            pltpu.VMEM((chips, CHAINS, rows, BD), f32),
            pltpu.VMEM((max(1, chips - 1), CHAINS, rows, BD), jnp.bfloat16),
            pltpu.VMEM((max(1, chips - 1), CHAINS, rows, BD), jnp.bfloat16),
            pltpu.VMEM((CHAINS, BD, BD), f32),
            pltpu.VMEM((CHAINS, BD, BD), f32),
            pltpu.VMEM((rows, BD), f32),
            dma((chips, CHAINS)),
            dma((chips, CHAINS)),
            dma((chips, CHAINS)),
            dma((max(1, chips - 1), CHAINS)),
            dma((max(1, chips - 1), CHAINS)),
            dma((CHAINS,)),
            dma((CHAINS,)),
        ],
        compiler_params=pltpu.CompilerParams(
            collective_id=0, has_side_effects=True, vmem_limit_bytes=48 * 2**20
        ),
        name="sweep",
    )(partial)


def eliminate(full, inverse):
    for first in range(0, PANEL, WIDTH):
        spread = [
            {
                j: jnp.broadcast_to(full[first + i][:, j:j + 1], full[0].shape)
                for j in range(first + i, PANEL)
            }
            for i in range(WIDTH)
        ]
        for i in range(WIDTH):
            row = first + i
            scale = lax.rsqrt(spread[i][row])
            full[row] = full[row] * scale
            inverse[row] = inverse[row] * scale
            for j in range(row + 1, PANEL):
                spread[i][j] = spread[i][j] * scale
            for later in range(i + 1, WIDTH):
                factor = spread[i][first + later]
                for j in range(first + later, PANEL):
                    spread[later][j] = spread[later][j] - factor * spread[i][j]
                full[first + later] = full[first + later] - factor * full[row]
                inverse[first + later] = inverse[first + later] - factor * inverse[row]
        for j in range(first + WIDTH, PANEL):
            for i in range(WIDTH):
                full[j] = full[j] - spread[i][j] * full[first + i]
                inverse[j] = inverse[j] - spread[i][j] * inverse[first + i]


def canonical_kernel(merged, x_in, g_in, top, bottom, upper, inverse):
    count = 2 * CHAINS
    eye = identity()
    for b in range(count):
        rows = pl.ds(b, BD, stride=count)
        upper[rows, :] = g_in[b] if b < CHAINS else x_in[b - CHAINS]
        inverse[rows, :] = eye

    @pl.loop(0, BD // PANEL)
    def _(panel):
        for known in range(1, BD // PANEL):
            @pl.when(panel == known)
            def _():
                lanes = slice(known * PANEL, (known + 1) * PANEL)
                for b in range(count):
                    done = pl.ds(b, known * PANEL, stride=count)
                    here = pl.ds(known * PANEL * count + b, PANEL, stride=count)
                    rows = upper[done, :]
                    upper[here, :] -= mm_tn(rows[:, lanes], rows)
                    if b < CHAINS:
                        inverse[here, :] -= mm_tn(rows[:, lanes], inverse[done, :])

        start = panel * PANEL * count
        where = lambda i: pl.ds(pl.multiple_of(start + i * count, count), count)
        ahead = lax.rem(BD - panel * PANEL, BD)
        full = [pltpu.roll(upper[where(i), :], ahead, 1) for i in range(PANEL)]
        inv = [inverse[where(i), :] for i in range(PANEL)]
        eliminate(full, inv)
        for i in range(PANEL):
            upper[where(i), :] = pltpu.roll(full[i], panel * PANEL, 1)
            inverse[where(i), :] = inv[i]

    lanes = lax.broadcasted_iota(jnp.int32, (BD, BD), 1)
    triangle = lanes >= lax.broadcasted_iota(jnp.int32, (BD, BD), 0)
    for k in range(CHAINS):
        lower_inv = inverse[pl.ds(k, BD, stride=count), :]
        carried = upper[pl.ds(CHAINS + k, BD, stride=count), :]
        carried = jnp.where(triangle, carried, 0.0)
        out = bottom if k % 2 else top
        for p in range(PH):
            part = mm_nt(lower_inv, merged[k, pl.ds(p * BD, BD), :])
            out[0, k // 2, :, pl.ds(p * BD, BD)] = mm_nt(part, carried)


def canonical(merged, x, gram):
    vmem = pl.BlockSpec(memory_space=pltpu.VMEM)
    out = jax.ShapeDtypeStruct((1, SEC_DEV, BD, PH * BD), jnp.float32)
    return pl.pallas_call(
        canonical_kernel,
        out_shape=(out, out),
        in_specs=[vmem, vmem, vmem],
        out_specs=(vmem, vmem),
        scratch_shapes=[
            pltpu.VMEM((2 * CHAINS * BD, BD), jnp.float32),
            pltpu.VMEM((2 * CHAINS * BD, BD), jnp.float32),
        ],
        compiler_params=pltpu.CompilerParams(vmem_limit_bytes=32 * 2**20),
        name="canonical",
    )(merged, x, gram)


def local(top_blocks, bottom_blocks, row_tensor, merge_owner, merge_sub):
    owners = lax.axis_size("sector")
    sites = lax.axis_size("site")
    sectors = owners * SEC_DEV
    target = merge_owner[0, :, 0] * SEC_DEV + merge_sub[0]
    partial = absorb(target, top_blocks, bottom_blocks, row_tensor, sectors)
    partial = partial.reshape(owners, CHAINS, PH * BD, BD)
    return canonical(*sweep(partial, sites, owners))


def solution(mesh):
    placed = (
        P("site", "sector", None, None),
        P("site", "sector", None, None),
        P("site", "sector", None, None),
        P("site", "sector", None),
        P("site", "sector"),
    )
    return jax.shard_map(
        local,
        mesh=mesh,
        in_specs=placed,
        out_specs=(P("site", "sector", None, None), P("site", "sector", None, None)),
        check_vma=False,
    )
```

```python
import functools

import jax
import jax.numpy as jnp
from jax import lax
from jax.experimental import pallas as pl
from jax.experimental.pallas import tpu as pltpu
from jax.sharding import PartitionSpec as P

PH = 4
BD = 128
SEC_DEV = 2
CHAINS = 4
PANEL = 32
WIDTH = 4


def absorb_kernel(owner, member, top, bottom, weights, partial):
    step = pl.program_id(0)

    @pl.when(step == 0)
    def _():
        partial[...] = jnp.zeros_like(partial)

    sector = owner[0, step, 0] * SEC_DEV + member[0, step]
    for boundary, blocks in enumerate((top, bottom)):
        absorbed = jnp.dot(blocks[0, 0], weights[0, 0], preferred_element_type=jnp.float32)
        partial[sector, boundary] += absorbed.astype(jnp.bfloat16).astype(jnp.float32)


def absorb(top_blocks, bottom_blocks, row_tensor, merge_owner, merge_sub, sectors):
    count, rows, inner = top_blocks.shape[1:]
    block = lambda *tail: pl.BlockSpec((1, 1) + tail, lambda j: (0, j, 0, 0))
    smem = pl.BlockSpec(memory_space=pltpu.SMEM)
    return pl.pallas_call(
        absorb_kernel,
        out_shape=jax.ShapeDtypeStruct((sectors, 2, rows, BD), jnp.float32),
        grid=(count,),
        in_specs=[smem, smem, block(rows, inner), block(rows, inner), block(inner, BD)],
        out_specs=pl.BlockSpec((sectors, 2, rows, BD), lambda j: (0, 0, 0, 0)),
        compiler_params=pltpu.CompilerParams(vmem_limit_bytes=48 * 2**20),
        name="absorb",
    )(merge_owner, merge_sub, top_blocks, bottom_blocks, row_tensor)


def split(value):
    high = value.astype(jnp.bfloat16)
    return high, (value - high.astype(jnp.float32)).astype(jnp.bfloat16)


def joined(axis, *parts):
    return jnp.concatenate(parts, axis=axis)


def dot3(a, b, a_axis, b_axis):
    a_high, a_low = split(a)
    b_high, b_low = split(b)
    return lax.dot_general(
        joined(a_axis, a_high, a_high, a_low), joined(b_axis, b_high, b_low, b_high),
        (((a_axis,), (b_axis,)), ((), ())), preferred_element_type=jnp.float32,
    )


def identity():
    return (
        lax.broadcasted_iota(jnp.int32, (BD, BD), 0) == lax.broadcasted_iota(jnp.int32, (BD, BD), 1)
    ).astype(jnp.float32)


def sweep_kernel(
    sites, owners, partial, m_out, x_out, g_out,
    own, near, away, landed, leaving, arriving, turned, turned_cat, merged_cat,
    own_sem, near_send, near_recv, away_send, away_recv, site_send, site_recv,
):
    chips = owners // 2
    site = lax.axis_index("site")
    sector = lax.axis_index("sector")
    core = sector % 2
    chip = sector // 2

    def at(site_to, sector_to):
        return (site_to, sector_to)

    partner = at(site, chip * 2 + (1 - core))

    def mate(shift):
        return at(site, ((chip + shift) % chips) * 2 + core)

    barrier = pltpu.get_barrier_semaphore()
    for device in [partner] + [mate(shift) for shift in range(1, chips)]:
        pl.semaphore_signal(barrier, inc=1, device_id=device, device_id_type=pl.DeviceIdType.MESH)

    @pl.when(site > 0)
    def _():
        pl.semaphore_signal(
            barrier, inc=1, device_id=at(site - 1, sector), device_id_type=pl.DeviceIdType.MESH
        )

    @pl.when(site < sites - 1)
    def _():
        pl.semaphore_signal(
            barrier, inc=1, device_id=at(site + 1, sector), device_id_type=pl.DeviceIdType.MESH
        )

    sides = jnp.where(site > 0, 1, 0) + jnp.where(site < sites - 1, 1, 0)
    pl.semaphore_wait(barrier, chips + sides)

    def own_copy(shift, k):
        owner = ((chip + shift) % chips) * 2 + core
        return pltpu.make_async_copy(partial.at[owner, k], own.at[shift, k], own_sem.at[shift, k])

    def near_copy(shift, k):
        owner = ((chip + shift) % chips) * 2 + (1 - core)
        return pltpu.make_async_remote_copy(
            src_ref=partial.at[owner, k], dst_ref=near.at[shift, k],
            send_sem=near_send.at[shift, k], recv_sem=near_recv.at[shift, k],
            device_id=partner, device_id_type=pl.DeviceIdType.MESH,
        )

    def away_copy(shift, k):
        return pltpu.make_async_remote_copy(
            src_ref=away.at[shift - 1, k], dst_ref=landed.at[shift - 1, k],
            send_sem=away_send.at[shift - 1, k], recv_sem=away_recv.at[shift - 1, k],
            device_id=mate(shift), device_id_type=pl.DeviceIdType.MESH,
        )

    def site_copy(k):
        return pltpu.make_async_remote_copy(
            src_ref=leaving.at[k], dst_ref=arriving.at[k],
            send_sem=site_send.at[k], recv_sem=site_recv.at[k],
            device_id=at(site + 1, sector), device_id_type=pl.DeviceIdType.MESH,
        )

    order = list(range(1, chips)) + [0]
    for shift in order:
        @pl.loop(0, CHAINS)
        def _(k):
            near_copy(shift, k).start()
            own_copy(shift, k).start()

    @pl.loop(0, CHAINS)
    def _(k):
        for shift in range(1, chips):
            near_copy(shift, k).wait_recv()
            own_copy(shift, k).wait()
            away[shift - 1, k] = (near[shift, k] + own[shift, k]).astype(jnp.bfloat16)
            away_copy(shift, k).start()

    eye = identity()

    @pl.loop(0, CHAINS)
    def _(k):
        near_copy(0, k).wait_recv()
        own_copy(0, k).wait()
        for shift in range(1, chips):
            away_copy(shift, k).wait_recv()
        for p in range(PH):
            rows = pl.ds(p * BD, BD)
            merged = near[0, k, rows, :] + own[0, k, rows, :]
            for shift in range(1, chips):
                merged += landed[shift - 1, k, rows, :].astype(jnp.float32)
            if p == 0:
                merged += eye
            m_out[k, rows, :] = merged
            turned[rows, :] = merged.T
            high, low = split(merged.T)
            turned_cat[rows, :] = joined(1, high, high, low)
            high, low = split(merged)
            merged_cat[pl.ds(p * 3 * BD, 3 * BD), :] = joined(0, high, low, high)

        @pl.when(site == 0)
        def _():
            x_out[k] = eye

        @pl.when(site > 0)
        def _():
            site_copy(k).wait_recv()
            x_out[k] = arriving[k]

        high, low = split(x_out[k])
        half = jnp.dot(
            turned_cat[...], joined(0, high, low, high), preferred_element_type=jnp.float32
        )
        high, low = split(half)
        cut = lambda part, p: part[p * BD:(p + 1) * BD]
        grams = []
        for p in range(PH):
            h, l = cut(high, p), cut(low, p)
            grams += [h, h, l]
        gram = jnp.dot(joined(1, *grams), merged_cat[...], preferred_element_type=jnp.float32)
        trace = jnp.sum(jnp.sum(half * turned[...], axis=0, keepdims=True), axis=1, keepdims=True)
        scale = 1.0 / (trace * (1.0 / (BD * BD)) + 1e-06)
        g_out[k] = gram

        @pl.when(site < sites - 1)
        def _():
            leaving[k] = gram * scale
            site_copy(k).start()

    @pl.loop(0, CHAINS)
    def _(k):
        for shift in range(chips):
            near_copy(shift, k).wait_send()
        for shift in range(1, chips):
            away_copy(shift, k).wait_send()

        @pl.when(site < sites - 1)
        def _():
            site_copy(k).wait_send()


def sweep(partial, sites, owners):
    chips = owners // 2
    rows = PH * BD
    vmem = pl.BlockSpec(memory_space=pltpu.VMEM)
    f32 = jnp.float32
    dma = pltpu.SemaphoreType.DMA
    return pl.pallas_call(
        functools.partial(sweep_kernel, sites, owners),
        out_shape=(
            jax.ShapeDtypeStruct((CHAINS, rows, BD), f32),
            jax.ShapeDtypeStruct((CHAINS, BD, BD), f32),
            jax.ShapeDtypeStruct((CHAINS, BD, BD), f32),
        ),
        in_specs=[pl.BlockSpec(memory_space=pl.ANY)],
        out_specs=(vmem, vmem, vmem),
        scratch_shapes=[
            pltpu.VMEM((chips, CHAINS, rows, BD), f32),
            pltpu.VMEM((chips, CHAINS, rows, BD), f32),
            pltpu.VMEM((max(1, chips - 1), CHAINS, rows, BD), jnp.bfloat16),
            pltpu.VMEM((max(1, chips - 1), CHAINS, rows, BD), jnp.bfloat16),
            pltpu.VMEM((CHAINS, BD, BD), f32),
            pltpu.VMEM((CHAINS, BD, BD), f32),
            pltpu.VMEM((rows, BD), f32),
            pltpu.VMEM((rows, 3 * BD), jnp.bfloat16),
            pltpu.VMEM((3 * rows, BD), jnp.bfloat16),
            dma((chips, CHAINS)),
            dma((chips, CHAINS)),
            dma((chips, CHAINS)),
            dma((max(1, chips - 1), CHAINS)),
            dma((max(1, chips - 1), CHAINS)),
            dma((CHAINS,)),
            dma((CHAINS,)),
        ],
        compiler_params=pltpu.CompilerParams(
            collective_id=0, has_side_effects=True, vmem_limit_bytes=48 * 2**20
        ),
        name="sweep",
    )(partial)


def eliminate(full, inverse):
    for first in range(0, PANEL, WIDTH):
        spread = [
            {
                j: jnp.broadcast_to(full[first + i][:, j:j + 1], full[0].shape)
                for j in range(first + i, PANEL)
            }
            for i in range(WIDTH)
        ]
        for i in range(WIDTH):
            row = first + i
            scale = lax.rsqrt(spread[i][row])
            full[row] = full[row] * scale
            inverse[row] = inverse[row] * scale
            for j in range(row + 1, PANEL):
                spread[i][j] = spread[i][j] * scale
            for later in range(i + 1, WIDTH):
                factor = spread[i][first + later]
                for j in range(first + later, PANEL):
                    spread[later][j] = spread[later][j] - factor * spread[i][j]
                full[first + later] = full[first + later] - factor * full[row]
                inverse[first + later] = inverse[first + later] - factor * inverse[row]
        for j in range(first + WIDTH, PANEL):
            for i in range(WIDTH):
                full[j] = full[j] - spread[i][j] * full[first + i]
                inverse[j] = inverse[j] - spread[i][j] * inverse[first + i]


def canonical_kernel(merged, x_in, g_in, top, bottom, upper, inverse):
    count = 2 * CHAINS
    eye = identity()
    for b in range(count):
        rows = pl.ds(b, BD, stride=count)
        upper[rows, :] = g_in[b] if b < CHAINS else x_in[b - CHAINS]
        inverse[rows, :] = eye

    @pl.loop(0, BD // PANEL)
    def _(panel):
        for known in range(1, BD // PANEL):
            @pl.when(panel == known)
            def _():
                lanes = slice(known * PANEL, (known + 1) * PANEL)
                for b in range(count):
                    done = pl.ds(b, known * PANEL, stride=count)
                    here = pl.ds(known * PANEL * count + b, PANEL, stride=count)
                    rows = upper[done, :]
                    upper[here, :] -= dot3(rows[:, lanes], rows, 0, 0)
                    if b < CHAINS:
                        inverse[here, :] -= dot3(rows[:, lanes], inverse[done, :], 0, 0)

        start = panel * PANEL * count
        where = lambda i: pl.ds(pl.multiple_of(start + i * count, count), count)
        ahead = lax.rem(BD - panel * PANEL, BD)
        full = [pltpu.roll(upper[where(i), :], ahead, 1) for i in range(PANEL)]
        inv = [inverse[where(i), :] for i in range(PANEL)]
        eliminate(full, inv)
        for i in range(PANEL):
            upper[where(i), :] = pltpu.roll(full[i], panel * PANEL, 1)
            inverse[where(i), :] = inv[i]

    lanes = lax.broadcasted_iota(jnp.int32, (BD, BD), 1)
    triangle = lanes >= lax.broadcasted_iota(jnp.int32, (BD, BD), 0)
    for k in range(CHAINS):
        lower_inv = inverse[pl.ds(k, BD, stride=count), :]
        carried = upper[pl.ds(CHAINS + k, BD, stride=count), :]
        carried = jnp.where(triangle, carried, 0.0)
        out = bottom if k % 2 else top
        for p in range(PH):
            part = dot3(lower_inv, merged[k, pl.ds(p * BD, BD), :], 1, 1)
            out[0, k // 2, :, pl.ds(p * BD, BD)] = dot3(part, carried, 1, 1)


def canonical(merged, x, gram):
    vmem = pl.BlockSpec(memory_space=pltpu.VMEM)
    out = jax.ShapeDtypeStruct((1, SEC_DEV, BD, PH * BD), jnp.float32)
    return pl.pallas_call(
        canonical_kernel,
        out_shape=(out, out),
        in_specs=[vmem, vmem, vmem],
        out_specs=(vmem, vmem),
        scratch_shapes=[
            pltpu.VMEM((2 * CHAINS * BD, BD), jnp.float32),
            pltpu.VMEM((2 * CHAINS * BD, BD), jnp.float32),
        ],
        compiler_params=pltpu.CompilerParams(vmem_limit_bytes=32 * 2**20),
        name="canonical",
    )(merged, x, gram)


def local(top_blocks, bottom_blocks, row_tensor, merge_owner, merge_sub):
    owners = lax.axis_size("sector")
    sites = lax.axis_size("site")
    sectors = owners * SEC_DEV
    partial = absorb(top_blocks, bottom_blocks, row_tensor, merge_owner, merge_sub, sectors)
    partial = partial.reshape(owners, CHAINS, PH * BD, BD)
    return canonical(*sweep(partial, sites, owners))


def solution(mesh):
    placed = (
        P("site", "sector", None, None),
        P("site", "sector", None, None),
        P("site", "sector", None, None),
        P("site", "sector", None),
        P("site", "sector"),
    )
    return jax.shard_map(
        local,
        mesh=mesh,
        in_specs=placed,
        out_specs=(P("site", "sector", None, None), P("site", "sector", None, None)),
        check_vma=False,
    )
```

```python
import functools

import jax
import jax.numpy as jnp
from jax import lax
from jax.experimental import pallas as pl
from jax.experimental.pallas import tpu as pltpu
from jax.sharding import PartitionSpec as P

PH = 4
BD = 128
SEC_DEV = 2
CHAINS = 4
PANEL = 32
WIDTH = 4


def split(value):
    high = value.astype(jnp.bfloat16)
    return high, (value - high.astype(jnp.float32)).astype(jnp.bfloat16)


def joined(axis, *parts):
    return jnp.concatenate(parts, axis=axis)


def dot3(a, b, a_axis, b_axis):
    a_high, a_low = split(a)
    b_high, b_low = split(b)
    return lax.dot_general(
        joined(a_axis, a_high, a_high, a_low), joined(b_axis, b_high, b_low, b_high),
        (((a_axis,), (b_axis,)), ((), ())), preferred_element_type=jnp.float32,
    )


def identity():
    return (
        lax.broadcasted_iota(jnp.int32, (BD, BD), 0) == lax.broadcasted_iota(jnp.int32, (BD, BD), 1)
    ).astype(jnp.float32)


def sweep_kernel(
    sites, owners, masks_in, tops_in, bottoms_in, weights_in, m_out, x_out, g_out,
    masks, blocks, weights, absorbed, own, leave_near, near, away, landed,
    leaving, arriving, turned, turned_cat, merged_cat,
    mask_sem, block_sem, weight_sem,
    near_send, near_recv, away_send, away_recv, site_send, site_recv,
):
    count = weights.shape[0]
    chips = owners // 2
    site = lax.axis_index("site")
    sector = lax.axis_index("sector")
    core = sector % 2
    chip = sector // 2

    def at(site_to, sector_to):
        return (site_to, sector_to)

    partner = at(site, chip * 2 + (1 - core))

    def mate(shift):
        return at(site, ((chip + shift) % chips) * 2 + core)

    mask_load = pltpu.make_async_copy(masks_in, masks, mask_sem)
    mask_load.start()

    def block_load(boundary, j):
        source = bottoms_in if boundary else tops_in
        return pltpu.make_async_copy(
            source.at[0, j], blocks.at[boundary, j], block_sem.at[boundary, j]
        )

    def weight_load(j):
        return pltpu.make_async_copy(weights_in.at[0, j], weights.at[j], weight_sem.at[j])

    @pl.loop(0, count)
    def _(j):
        weight_load(j).start()
        block_load(0, j).start()

    @pl.loop(0, count)
    def _(j):
        block_load(1, j).start()

    barrier = pltpu.get_barrier_semaphore()
    for device in [partner] + [mate(shift) for shift in range(1, chips)]:
        pl.semaphore_signal(barrier, inc=1, device_id=device, device_id_type=pl.DeviceIdType.MESH)

    @pl.when(site > 0)
    def _():
        pl.semaphore_signal(
            barrier, inc=1, device_id=at(site - 1, sector), device_id_type=pl.DeviceIdType.MESH
        )

    @pl.when(site < sites - 1)
    def _():
        pl.semaphore_signal(
            barrier, inc=1, device_id=at(site + 1, sector), device_id_type=pl.DeviceIdType.MESH
        )

    sides = jnp.where(site > 0, 1, 0) + jnp.where(site < sites - 1, 1, 0)
    def near_copy(shift, k):
        return pltpu.make_async_remote_copy(
            src_ref=leave_near.at[shift, k], dst_ref=near.at[shift, k],
            send_sem=near_send.at[shift, k], recv_sem=near_recv.at[shift, k],
            device_id=partner, device_id_type=pl.DeviceIdType.MESH,
        )

    def away_copy(shift, k):
        return pltpu.make_async_remote_copy(
            src_ref=away.at[shift - 1, k], dst_ref=landed.at[shift - 1, k],
            send_sem=away_send.at[shift - 1, k], recv_sem=away_recv.at[shift - 1, k],
            device_id=mate(shift), device_id_type=pl.DeviceIdType.MESH,
        )

    def site_copy(k):
        return pltpu.make_async_remote_copy(
            src_ref=leaving.at[k], dst_ref=arriving.at[k],
            send_sem=site_send.at[k], recv_sem=site_recv.at[k],
            device_id=at(site + 1, sector), device_id_type=pl.DeviceIdType.MESH,
        )

    def combine(boundary, shift, core_to, out):
        owner = ((chip + shift) % chips) * 2 + core_to
        picks = [
            [masks[owner * SEC_DEV + sub, j] for j in range(count)] for sub in range(SEC_DEV)
        ]

        @pl.loop(0, PH * BD // 16, unroll=2)
        def _(tile):
            rows = pl.ds(pl.multiple_of(tile * 16, 16), 16)
            parts = [absorbed[j, rows, :].astype(jnp.float32) for j in range(count)]
            for sub in range(SEC_DEV):
                sums = []
                for half in (slice(0, 8), slice(8, 16)):
                    terms = [picks[sub][j] * parts[j][half] for j in range(count)]
                    while len(terms) > 1:
                        terms = [sum(terms[i:i + 2]) for i in range(0, len(terms), 2)]
                    sums.append(terms[0])
                total = jnp.concatenate(sums, axis=0)
                out[shift, boundary * SEC_DEV + sub, rows, :] = total.astype(out.dtype)

    order = list(range(1, chips)) + [0]
    for boundary in range(2):
        @pl.loop(0, count)
        def _(j):
            if boundary == 0:
                weight_load(j).wait()
            block_load(boundary, j).wait()
            absorbed[j] = jnp.dot(
                blocks[boundary, j], weights[j], preferred_element_type=jnp.float32
            ).astype(jnp.bfloat16)

        if boundary == 0:
            mask_load.wait()
            pl.semaphore_wait(barrier, chips + sides)
        for shift in order:
            combine(boundary, shift, 1 - core, leave_near)
            for sub in range(SEC_DEV):
                near_copy(shift, boundary * SEC_DEV + sub).start()
        for shift in order:
            combine(boundary, shift, core, own)
            if shift:
                for sub in range(SEC_DEV):
                    k = boundary * SEC_DEV + sub
                    near_copy(shift, k).wait_recv()
                    away[shift - 1, k] = (
                        near[shift, k].astype(jnp.float32) + own[shift, k]
                    ).astype(jnp.bfloat16)
                    away_copy(shift, k).start()

    eye = identity()

    @pl.loop(0, CHAINS)
    def _(k):
        near_copy(0, k).wait_recv()
        for shift in range(1, chips):
            away_copy(shift, k).wait_recv()
        for p in range(PH):
            rows = pl.ds(p * BD, BD)
            merged = near[0, k, rows, :].astype(jnp.float32) + own[0, k, rows, :]
            for shift in range(1, chips):
                merged += landed[shift - 1, k, rows, :].astype(jnp.float32)
            if p == 0:
                merged += eye
            m_out[k, rows, :] = merged
            turned[rows, :] = merged.T
            high, low = split(merged.T)
            turned_cat[rows, :] = joined(1, high, high, low)
            high, low = split(merged)
            merged_cat[pl.ds(p * 3 * BD, 3 * BD), :] = joined(0, high, low, high)

        @pl.when(site == 0)
        def _():
            x_out[k] = eye

        @pl.when(site > 0)
        def _():
            site_copy(k).wait_recv()
            x_out[k] = arriving[k]

        high, low = split(x_out[k])
        half = jnp.dot(
            turned_cat[...], joined(0, high, low, high), preferred_element_type=jnp.float32
        )
        high, low = split(half)
        cut = lambda part, p: part[p * BD:(p + 1) * BD]
        grams = []
        for p in range(PH):
            h, l = cut(high, p), cut(low, p)
            grams += [h, h, l]
        gram = jnp.dot(joined(1, *grams), merged_cat[...], preferred_element_type=jnp.float32)
        trace = jnp.sum(jnp.sum(half * turned[...], axis=0, keepdims=True), axis=1, keepdims=True)
        scale = 1.0 / (trace * (1.0 / (BD * BD)) + 1e-06)
        g_out[k] = gram

        @pl.when(site < sites - 1)
        def _():
            leaving[k] = gram * scale
            site_copy(k).start()

    @pl.loop(0, CHAINS)
    def _(k):
        for shift in range(chips):
            near_copy(shift, k).wait_send()
        for shift in range(1, chips):
            away_copy(shift, k).wait_send()

        @pl.when(site < sites - 1)
        def _():
            site_copy(k).wait_send()


def sweep(masks, top_blocks, bottom_blocks, row_tensor, sites, owners):
    chips = owners // 2
    count, _, inner = top_blocks.shape[1:]
    rows = PH * BD
    vmem = pl.BlockSpec(memory_space=pltpu.VMEM)
    f32 = jnp.float32
    dma = pltpu.SemaphoreType.DMA
    return pl.pallas_call(
        functools.partial(sweep_kernel, sites, owners),
        out_shape=(
            jax.ShapeDtypeStruct((CHAINS, rows, BD), f32),
            jax.ShapeDtypeStruct((CHAINS, BD, BD), f32),
            jax.ShapeDtypeStruct((CHAINS, BD, BD), f32),
        ),
        in_specs=[pl.BlockSpec(memory_space=pl.ANY)] * 4,
        out_specs=(vmem, vmem, vmem),
        scratch_shapes=[
            pltpu.VMEM(masks.shape, f32),
            pltpu.VMEM((2, count, rows, inner), jnp.bfloat16),
            pltpu.VMEM((count, inner, BD), jnp.bfloat16),
            pltpu.VMEM((count, rows, BD), jnp.bfloat16),
            pltpu.VMEM((chips, CHAINS, rows, BD), f32),
            pltpu.VMEM((chips, CHAINS, rows, BD), jnp.bfloat16),
            pltpu.VMEM((chips, CHAINS, rows, BD), jnp.bfloat16),
            pltpu.VMEM((max(1, chips - 1), CHAINS, rows, BD), jnp.bfloat16),
            pltpu.VMEM((max(1, chips - 1), CHAINS, rows, BD), jnp.bfloat16),
            pltpu.VMEM((CHAINS, BD, BD), f32),
            pltpu.VMEM((CHAINS, BD, BD), f32),
            pltpu.VMEM((rows, BD), f32),
            pltpu.VMEM((rows, 3 * BD), jnp.bfloat16),
            pltpu.VMEM((3 * rows, BD), jnp.bfloat16),
            dma(()),
            dma((2, count)),
            dma((count,)),
            dma((chips, CHAINS)),
            dma((chips, CHAINS)),
            dma((max(1, chips - 1), CHAINS)),
            dma((max(1, chips - 1), CHAINS)),
            dma((CHAINS,)),
            dma((CHAINS,)),
        ],
        compiler_params=pltpu.CompilerParams(
            collective_id=0, has_side_effects=True, vmem_limit_bytes=48 * 2**20
        ),
        name="sweep",
    )(masks, top_blocks, bottom_blocks, row_tensor)


def eliminate(full, inverse):
    for first in range(0, PANEL, WIDTH):
        spread = [
            {
                j: jnp.broadcast_to(full[first + i][:, j:j + 1], full[0].shape)
                for j in range(first + i, PANEL)
            }
            for i in range(WIDTH)
        ]
        for i in range(WIDTH):
            row = first + i
            scale = lax.rsqrt(spread[i][row])
            full[row] = full[row] * scale
            inverse[row] = inverse[row] * scale
            for j in range(row + 1, PANEL):
                spread[i][j] = spread[i][j] * scale
            for later in range(i + 1, WIDTH):
                factor = spread[i][first + later]
                for j in range(first + later, PANEL):
                    spread[later][j] = spread[later][j] - factor * spread[i][j]
                full[first + later] = full[first + later] - factor * full[row]
                inverse[first + later] = inverse[first + later] - factor * inverse[row]
        for j in range(first + WIDTH, PANEL):
            for i in range(WIDTH):
                full[j] = full[j] - spread[i][j] * full[first + i]
                inverse[j] = inverse[j] - spread[i][j] * inverse[first + i]


def canonical_kernel(merged, x_in, g_in, top, bottom, upper, inverse):
    count = 2 * CHAINS
    eye = identity()
    for b in range(count):
        rows = pl.ds(b, BD, stride=count)
        upper[rows, :] = g_in[b] if b < CHAINS else x_in[b - CHAINS]
        inverse[rows, :] = eye

    @pl.loop(0, BD // PANEL)
    def _(panel):
        for known in range(1, BD // PANEL):
            @pl.when(panel == known)
            def _():
                lanes = slice(known * PANEL, (known + 1) * PANEL)
                for b in range(count):
                    done = pl.ds(b, known * PANEL, stride=count)
                    here = pl.ds(known * PANEL * count + b, PANEL, stride=count)
                    rows = upper[done, :]
                    upper[here, :] -= dot3(rows[:, lanes], rows, 0, 0)
                    if b < CHAINS:
                        inverse[here, :] -= dot3(rows[:, lanes], inverse[done, :], 0, 0)

        start = panel * PANEL * count
        where = lambda i: pl.ds(pl.multiple_of(start + i * count, count), count)
        ahead = lax.rem(BD - panel * PANEL, BD)
        full = [pltpu.roll(upper[where(i), :], ahead, 1) for i in range(PANEL)]
        inv = [inverse[where(i), :] for i in range(PANEL)]
        eliminate(full, inv)
        for i in range(PANEL):
            upper[where(i), :] = pltpu.roll(full[i], panel * PANEL, 1)
            inverse[where(i), :] = inv[i]

    lanes = lax.broadcasted_iota(jnp.int32, (BD, BD), 1)
    triangle = lanes >= lax.broadcasted_iota(jnp.int32, (BD, BD), 0)
    for k in range(CHAINS):
        lower_inv = inverse[pl.ds(k, BD, stride=count), :]
        carried = upper[pl.ds(CHAINS + k, BD, stride=count), :]
        carried = jnp.where(triangle, carried, 0.0)
        out = bottom if k // SEC_DEV else top
        for p in range(PH):
            part = dot3(lower_inv, merged[k, pl.ds(p * BD, BD), :], 1, 1)
            out[0, k % SEC_DEV, :, pl.ds(p * BD, BD)] = dot3(part, carried, 1, 1)


def canonical(merged, x, gram):
    vmem = pl.BlockSpec(memory_space=pltpu.VMEM)
    out = jax.ShapeDtypeStruct((1, SEC_DEV, BD, PH * BD), jnp.float32)
    return pl.pallas_call(
        canonical_kernel,
        out_shape=(out, out),
        in_specs=[vmem, vmem, vmem],
        out_specs=(vmem, vmem),
        scratch_shapes=[
            pltpu.VMEM((2 * CHAINS * BD, BD), jnp.float32),
            pltpu.VMEM((2 * CHAINS * BD, BD), jnp.float32),
        ],
        compiler_params=pltpu.CompilerParams(vmem_limit_bytes=32 * 2**20),
        name="canonical",
    )(merged, x, gram)


def local(top_blocks, bottom_blocks, row_tensor, merge_owner, merge_sub):
    owners = lax.axis_size("sector")
    sites = lax.axis_size("site")
    sectors = owners * SEC_DEV
    target = merge_owner[0, :, 0] * SEC_DEV + merge_sub[0]
    masks = (jnp.arange(sectors, dtype=jnp.int32)[:, None] == target[None, :]).astype(jnp.float32)
    masks = jnp.broadcast_to(masks[:, :, None, None], masks.shape + (8, BD))
    return canonical(*sweep(masks, top_blocks, bottom_blocks, row_tensor, sites, owners))


def solution(mesh):
    placed = (
        P("site", "sector", None, None),
        P("site", "sector", None, None),
        P("site", "sector", None, None),
        P("site", "sector", None),
        P("site", "sector"),
    )
    return jax.shard_map(
        local,
        mesh=mesh,
        in_specs=placed,
        out_specs=(P("site", "sector", None, None), P("site", "sector", None, None)),
        check_vma=False,
    )
```

```python
import functools

import jax
import jax.numpy as jnp
from jax import lax
from jax.experimental import pallas as pl
from jax.experimental.pallas import tpu as pltpu
from jax.sharding import PartitionSpec as P

PH = 4
BD = 128
SEC_DEV = 2
CHAINS = 4
PANEL = 32
WIDTH = 4


def split(value):
    high = value.astype(jnp.bfloat16)
    return high, (value - high.astype(jnp.float32)).astype(jnp.bfloat16)


def joined(axis, *parts):
    return jnp.concatenate(parts, axis=axis)


def dot3(a, b, a_axis, b_axis):
    a_high, a_low = split(a)
    b_high, b_low = split(b)
    return lax.dot_general(
        joined(a_axis, a_high, a_high, a_low), joined(b_axis, b_high, b_low, b_high),
        (((a_axis,), (b_axis,)), ((), ())), preferred_element_type=jnp.float32,
    )


def identity():
    return (
        lax.broadcasted_iota(jnp.int32, (BD, BD), 0) == lax.broadcasted_iota(jnp.int32, (BD, BD), 1)
    ).astype(jnp.float32)


def sweep_kernel(
    sites, owners, masks_in, tops_in, bottoms_in, weights_in, m_out, x_out, g_out,
    masks, blocks, weights, absorbed, own, leave_near, near, away, landed,
    leaving, arriving, turned, turned_cat, merged_cat,
    mask_sem, block_sem, weight_sem,
    near_send, near_recv, away_send, away_recv, site_send, site_recv,
):
    count = weights.shape[0]
    chips = owners // 2
    site = lax.axis_index("site")
    sector = lax.axis_index("sector")
    core = sector % 2
    chip = sector // 2

    def at(site_to, sector_to):
        return (site_to, sector_to)

    partner = at(site, chip * 2 + (1 - core))

    def mate(shift):
        return at(site, ((chip + shift) % chips) * 2 + core)

    mask_load = pltpu.make_async_copy(masks_in, masks, mask_sem)
    mask_load.start()

    def block_load(boundary, j):
        source = bottoms_in if boundary else tops_in
        return pltpu.make_async_copy(
            source.at[0, j], blocks.at[boundary, j], block_sem.at[boundary, j]
        )

    def weight_load(j):
        return pltpu.make_async_copy(weights_in.at[0, j], weights.at[j], weight_sem.at[j])

    @pl.loop(0, count)
    def _(j):
        weight_load(j).start()
        block_load(0, j).start()

    @pl.loop(0, count)
    def _(j):
        block_load(1, j).start()

    barrier = pltpu.get_barrier_semaphore()
    for device in [partner] + [mate(shift) for shift in range(1, chips)]:
        pl.semaphore_signal(barrier, inc=1, device_id=device, device_id_type=pl.DeviceIdType.MESH)

    @pl.when(site > 0)
    def _():
        pl.semaphore_signal(
            barrier, inc=1, device_id=at(site - 1, sector), device_id_type=pl.DeviceIdType.MESH
        )

    @pl.when(site < sites - 1)
    def _():
        pl.semaphore_signal(
            barrier, inc=1, device_id=at(site + 1, sector), device_id_type=pl.DeviceIdType.MESH
        )

    sides = jnp.where(site > 0, 1, 0) + jnp.where(site < sites - 1, 1, 0)
    def near_copy(shift, k):
        return pltpu.make_async_remote_copy(
            src_ref=leave_near.at[shift, k], dst_ref=near.at[shift, k],
            send_sem=near_send.at[shift, k], recv_sem=near_recv.at[shift, k],
            device_id=partner, device_id_type=pl.DeviceIdType.MESH,
        )

    def away_copy(shift, k):
        return pltpu.make_async_remote_copy(
            src_ref=away.at[shift - 1, k], dst_ref=landed.at[shift - 1, k],
            send_sem=away_send.at[shift - 1, k], recv_sem=away_recv.at[shift - 1, k],
            device_id=mate(shift), device_id_type=pl.DeviceIdType.MESH,
        )

    def site_copy(k):
        return pltpu.make_async_remote_copy(
            src_ref=leaving.at[k], dst_ref=arriving.at[k],
            send_sem=site_send.at[k], recv_sem=site_recv.at[k],
            device_id=at(site + 1, sector), device_id_type=pl.DeviceIdType.MESH,
        )

    def combine(boundary, shift, core_to, out):
        owner = ((chip + shift) % chips) * 2 + core_to
        picks = [
            [masks[owner * SEC_DEV + sub, j] for j in range(count)] for sub in range(SEC_DEV)
        ]

        @pl.loop(0, PH * BD // 16, unroll=2)
        def _(tile):
            rows = pl.ds(pl.multiple_of(tile * 16, 16), 16)
            parts = [absorbed[j, rows, :].astype(jnp.float32) for j in range(count)]
            for sub in range(SEC_DEV):
                sums = []
                for half in (slice(0, 8), slice(8, 16)):
                    terms = [picks[sub][j] * parts[j][half] for j in range(count)]
                    while len(terms) > 1:
                        terms = [sum(terms[i:i + 2]) for i in range(0, len(terms), 2)]
                    sums.append(terms[0])
                total = jnp.concatenate(sums, axis=0)
                out[shift, boundary * SEC_DEV + sub, rows, :] = total.astype(out.dtype)

    order = list(range(1, chips)) + [0]
    for boundary in range(2):
        @pl.loop(0, count)
        def _(j):
            if boundary == 0:
                weight_load(j).wait()
            block_load(boundary, j).wait()
            absorbed[j] = jnp.dot(
                blocks[boundary, j], weights[j], preferred_element_type=jnp.float32
            ).astype(jnp.bfloat16)

        if boundary == 0:
            mask_load.wait()
            pl.semaphore_wait(barrier, chips + sides)
        for shift in order:
            combine(boundary, shift, 1 - core, leave_near)
            for sub in range(SEC_DEV):
                near_copy(shift, boundary * SEC_DEV + sub).start()
            combine(boundary, shift, core, own)
            if shift:
                for sub in range(SEC_DEV):
                    k = boundary * SEC_DEV + sub
                    near_copy(shift, k).wait_recv()
                    away[shift - 1, k] = (
                        near[shift, k].astype(jnp.float32) + own[shift, k]
                    ).astype(jnp.bfloat16)
                    away_copy(shift, k).start()

    eye = identity()

    @pl.loop(0, CHAINS)
    def _(k):
        near_copy(0, k).wait_recv()
        for shift in range(1, chips):
            away_copy(shift, k).wait_recv()
        for p in range(PH):
            rows = pl.ds(p * BD, BD)
            merged = near[0, k, rows, :].astype(jnp.float32) + own[0, k, rows, :]
            for shift in range(1, chips):
                merged += landed[shift - 1, k, rows, :].astype(jnp.float32)
            if p == 0:
                merged += eye
            m_out[k, rows, :] = merged
            turned[rows, :] = merged.T
            high, low = split(merged.T)
            turned_cat[rows, :] = joined(1, high, high, low)
            high, low = split(merged)
            merged_cat[pl.ds(p * 3 * BD, 3 * BD), :] = joined(0, high, low, high)

        @pl.when(site == 0)
        def _():
            x_out[k] = eye

        @pl.when(site > 0)
        def _():
            site_copy(k).wait_recv()
            x_out[k] = arriving[k]

        high, low = split(x_out[k])
        half = jnp.dot(
            turned_cat[...], joined(0, high, low, high), preferred_element_type=jnp.float32
        )
        high, low = split(half)
        cut = lambda part, p: part[p * BD:(p + 1) * BD]
        grams = []
        for p in range(PH):
            h, l = cut(high, p), cut(low, p)
            grams += [h, h, l]
        gram = jnp.dot(joined(1, *grams), merged_cat[...], preferred_element_type=jnp.float32)
        trace = jnp.sum(jnp.sum(half * turned[...], axis=0, keepdims=True), axis=1, keepdims=True)
        scale = 1.0 / (trace * (1.0 / (BD * BD)) + 1e-06)
        g_out[k] = gram

        @pl.when(site < sites - 1)
        def _():
            leaving[k] = gram * scale
            site_copy(k).start()

    @pl.loop(0, CHAINS)
    def _(k):
        for shift in range(chips):
            near_copy(shift, k).wait_send()
        for shift in range(1, chips):
            away_copy(shift, k).wait_send()

        @pl.when(site < sites - 1)
        def _():
            site_copy(k).wait_send()


def sweep(masks, top_blocks, bottom_blocks, row_tensor, sites, owners):
    chips = owners // 2
    count, _, inner = top_blocks.shape[1:]
    rows = PH * BD
    vmem = pl.BlockSpec(memory_space=pltpu.VMEM)
    f32 = jnp.float32
    dma = pltpu.SemaphoreType.DMA
    return pl.pallas_call(
        functools.partial(sweep_kernel, sites, owners),
        out_shape=(
            jax.ShapeDtypeStruct((CHAINS, rows, BD), f32),
            jax.ShapeDtypeStruct((CHAINS, BD, BD), f32),
            jax.ShapeDtypeStruct((CHAINS, BD, BD), f32),
        ),
        in_specs=[pl.BlockSpec(memory_space=pl.ANY)] + [pl.BlockSpec(memory_space=pltpu.HBM)] * 3,
        out_specs=(vmem, vmem, vmem),
        scratch_shapes=[
            pltpu.VMEM(masks.shape, f32),
            pltpu.VMEM((2, count, rows, inner), jnp.bfloat16),
            pltpu.VMEM((count, inner, BD), jnp.bfloat16),
            pltpu.VMEM((count, rows, BD), jnp.bfloat16),
            pltpu.VMEM((chips, CHAINS, rows, BD), f32),
            pltpu.VMEM((chips, CHAINS, rows, BD), jnp.bfloat16),
            pltpu.VMEM((chips, CHAINS, rows, BD), jnp.bfloat16),
            pltpu.VMEM((max(1, chips - 1), CHAINS, rows, BD), jnp.bfloat16),
            pltpu.VMEM((max(1, chips - 1), CHAINS, rows, BD), jnp.bfloat16),
            pltpu.VMEM((CHAINS, BD, BD), f32),
            pltpu.VMEM((CHAINS, BD, BD), f32),
            pltpu.VMEM((rows, BD), f32),
            pltpu.VMEM((rows, 3 * BD), jnp.bfloat16),
            pltpu.VMEM((3 * rows, BD), jnp.bfloat16),
            dma(()),
            dma((2, count)),
            dma((count,)),
            dma((chips, CHAINS)),
            dma((chips, CHAINS)),
            dma((max(1, chips - 1), CHAINS)),
            dma((max(1, chips - 1), CHAINS)),
            dma((CHAINS,)),
            dma((CHAINS,)),
        ],
        compiler_params=pltpu.CompilerParams(
            collective_id=0, has_side_effects=True, vmem_limit_bytes=48 * 2**20
        ),
        name="sweep",
    )(masks, top_blocks, bottom_blocks, row_tensor)


def eliminate(full, inverse):
    for first in range(0, PANEL, WIDTH):
        spread = [
            {
                j: jnp.broadcast_to(full[first + i][:, j:j + 1], full[0].shape)
                for j in range(first + i, PANEL)
            }
            for i in range(WIDTH)
        ]
        for i in range(WIDTH):
            row = first + i
            scale = lax.rsqrt(spread[i][row])
            full[row] = full[row] * scale
            inverse[row] = inverse[row] * scale
            for j in range(row + 1, PANEL):
                spread[i][j] = spread[i][j] * scale
            for later in range(i + 1, WIDTH):
                factor = spread[i][first + later]
                for j in range(first + later, PANEL):
                    spread[later][j] = spread[later][j] - factor * spread[i][j]
                full[first + later] = full[first + later] - factor * full[row]
                inverse[first + later] = inverse[first + later] - factor * inverse[row]
        for j in range(first + WIDTH, PANEL):
            for i in range(WIDTH):
                full[j] = full[j] - spread[i][j] * full[first + i]
                inverse[j] = inverse[j] - spread[i][j] * inverse[first + i]


def canonical_kernel(merged, x_in, g_in, top, bottom, upper, inverse):
    count = 2 * CHAINS
    eye = identity()
    for b in range(count):
        rows = pl.ds(b, BD, stride=count)
        upper[rows, :] = g_in[b] if b < CHAINS else x_in[b - CHAINS]
        inverse[rows, :] = eye

    @pl.loop(0, BD // PANEL)
    def _(panel):
        for known in range(1, BD // PANEL):
            @pl.when(panel == known)
            def _():
                lanes = slice(known * PANEL, (known + 1) * PANEL)
                for b in range(count):
                    done = pl.ds(b, known * PANEL, stride=count)
                    here = pl.ds(known * PANEL * count + b, PANEL, stride=count)
                    rows = upper[done, :]
                    upper[here, :] -= dot3(rows[:, lanes], rows, 0, 0)
                    if b < CHAINS:
                        inverse[here, :] -= dot3(rows[:, lanes], inverse[done, :], 0, 0)

        start = panel * PANEL * count
        where = lambda i: pl.ds(pl.multiple_of(start + i * count, count), count)
        ahead = lax.rem(BD - panel * PANEL, BD)
        full = [pltpu.roll(upper[where(i), :], ahead, 1) for i in range(PANEL)]
        inv = [inverse[where(i), :] for i in range(PANEL)]
        eliminate(full, inv)
        for i in range(PANEL):
            upper[where(i), :] = pltpu.roll(full[i], panel * PANEL, 1)
            inverse[where(i), :] = inv[i]

    lanes = lax.broadcasted_iota(jnp.int32, (BD, BD), 1)
    triangle = lanes >= lax.broadcasted_iota(jnp.int32, (BD, BD), 0)
    for k in range(CHAINS):
        lower_inv = inverse[pl.ds(k, BD, stride=count), :]
        carried = upper[pl.ds(CHAINS + k, BD, stride=count), :]
        carried = jnp.where(triangle, carried, 0.0)
        out = bottom if k // SEC_DEV else top
        part = dot3(lower_inv, merged[k], 1, 1)
        part = joined(0, *[part[:, p * BD:(p + 1) * BD] for p in range(PH)])
        part = dot3(part, carried, 1, 1)
        for p in range(PH):
            out[0, k % SEC_DEV, :, pl.ds(p * BD, BD)] = part[p * BD:(p + 1) * BD]


def canonical(merged, x, gram):
    vmem = pl.BlockSpec(memory_space=pltpu.VMEM)
    out = jax.ShapeDtypeStruct((1, SEC_DEV, BD, PH * BD), jnp.float32)
    return pl.pallas_call(
        canonical_kernel,
        out_shape=(out, out),
        in_specs=[vmem, vmem, vmem],
        out_specs=(vmem, vmem),
        scratch_shapes=[
            pltpu.VMEM((2 * CHAINS * BD, BD), jnp.float32),
            pltpu.VMEM((2 * CHAINS * BD, BD), jnp.float32),
        ],
        compiler_params=pltpu.CompilerParams(vmem_limit_bytes=32 * 2**20),
        name="canonical",
    )(merged, x, gram)


def local(top_blocks, bottom_blocks, row_tensor, merge_owner, merge_sub):
    owners = lax.axis_size("sector")
    sites = lax.axis_size("site")
    sectors = owners * SEC_DEV
    target = merge_owner[0, :, 0] * SEC_DEV + merge_sub[0]
    masks = (jnp.arange(sectors, dtype=jnp.int32)[:, None] == target[None, :]).astype(jnp.float32)
    masks = jnp.broadcast_to(masks[:, :, None, None], masks.shape + (8, BD))
    return canonical(*sweep(masks, top_blocks, bottom_blocks, row_tensor, sites, owners))


def solution(mesh):
    placed = (
        P("site", "sector", None, None),
        P("site", "sector", None, None),
        P("site", "sector", None, None),
        P("site", "sector", None),
        P("site", "sector"),
    )
    return jax.shard_map(
        local,
        mesh=mesh,
        in_specs=placed,
        out_specs=(P("site", "sector", None, None), P("site", "sector", None, None)),
        check_vma=False,
    )
```
